128 devices in a mesh: row: 16 (over z, x), col: 8 (over y, core).
Axes of the slice: x: 4, y: 4, z: 4, core: 2. Of those that a mesh axis runs over, the one named last changes fastest.
Arguments:
- features: float32 [32, 49152], P(None, ('row', 'col')), may hold values from -6 to 6
- lengthscale: float32 [32], replicated, may hold values from 1.5 to 6
- targets: float32 [64, 49152], P(None, ('row', 'col')), may hold values from -15 to 15, as said below
- mask: int32 [64, 49152], P(None, ('row', 'col')), may hold values from 0 to 1, as said below
Outputs:
- solution: float32 [64, 49152], P(None, ('row', 'col'))
- residual: float32 [64, 49152], P(None, ('row', 'col'))
The draws below stay inside these ranges and needn't reach their ends.
Inputs may be any that keep to these rules, and one draw needn't show every extreme that they name: `targets`: values scaled per configuration. `mask`: for each configuration the observed epochs are a prefix of 1 to 64 epochs; some configuration has all 64.
All inputs are finite; a program needn't handle non-finite values.
Results may differ from the reference program's by a relative error of at most 0.013.
Values may be sent and summed in bfloat16 or wider, within the bound.
No kernel may reach another device: no remote copies, remote signals or barrier semaphores. Data moves between devices by JAX's collectives and lax.ppermute only.
A program may use at most 64 MiB of HBM per device.

```python
import math
import jax
import jax.numpy as jnp
from jax import lax

F = 32
E = 64
ITERS = 2
N = 49152


def group_members(key):
    group_size = max(1, 2 * math.isqrt(N))
    groups_total = max(1, N // group_size)
    members = jax.random.randint(jax.random.fold_in(key, 101), (N,), 0, groups_total)
    return (members, groups_total)


def draw_features(key, part):
    members, groups_total = group_members(key)
    key = jax.random.fold_in(key, 7)
    key_centre, key_jitter = jax.random.split(key, 2)
    centres = jnp.clip(jax.random.normal(key_centre, (F, groups_total), jnp.float32), -4.5, 4.5)
    jitter = 0.25 * jax.random.normal(key_jitter, (F, N), jnp.float32)
    return centres[:, members] + jnp.clip(jitter, -1.0, 1.0)


def draw_targets(key, part):
    members, groups_total = group_members(key)
    key = jax.random.fold_in(key, 11)
    key_base, key_scale, key_shared, key_sign = jax.random.split(key, 4)
    position = jnp.arange(N).astype(jnp.float32) / N
    row_scale = jnp.exp(jax.random.uniform(key_scale, (N,), jnp.float32, 0.0, math.log(10.0))) / 4.0
    epochs = jnp.arange(E, dtype=jnp.int32)
    alternate = (1 - 2 * (epochs % 2)).astype(jnp.float32)
    rough = jax.random.uniform(key_shared, (E, groups_total), jnp.float32, 0.5, 1.5)
    group_sign = (2 * jax.random.randint(key_sign, (groups_total,), 0, 2) - 1).astype(jnp.float32)
    shared = alternate[:, None] * rough * group_sign[None, :]
    shared = shared[:, members]
    base = jnp.clip(jax.random.normal(key_base, (E, N), jnp.float32), -4.0, 4.0)
    ramp = 0.5 + position
    return (shared + 0.5 * base) * (ramp * row_scale)[None, :]


def draw_mask(key, part):
    key = jax.random.fold_in(key, 5)
    lengths = jax.random.randint(key, (N,), 1, E + 1)
    lengths = lengths.at[0].set(E)
    epochs = jnp.arange(E, dtype=jnp.int32)
    return (epochs[:, None] < lengths[None, :]).astype(jnp.int32)


def setup_inputs(seed: int = 0) -> dict:
    key_of = jax.random.split(jax.random.key(seed), 5)
    features = draw_features(jax.random.fold_in(key_of[4], 71), 0)
    lengthscale = jnp.clip(jnp.exp(jax.random.uniform(key_of[1], (F,), jnp.float32, math.log(1.5), math.log(6.0))), 1.5, 6.0)
    targets = draw_targets(jax.random.fold_in(key_of[4], 71), 0)
    mask = draw_mask(jax.random.fold_in(key_of[4], 71), 0)
    return dict(features=features, lengthscale=lengthscale, targets=targets, mask=mask)


noise_level = 0.5

def epoch_kernel():
    grid = jnp.arange(E).astype(jnp.float32)
    signal = 8.0 / math.sqrt(N)
    return signal * jnp.exp(-jnp.abs(grid[:, None] - grid[None, :]) / (E / 4.0))

def reference(features, lengthscale, targets, mask):
    observed = mask.astype(jnp.float32)
    scaled = features / lengthscale[:, None]
    sqnorm = lax.optimization_barrier(jnp.sum(scaled * scaled, axis=0))
    width = math.gcd(N, 1024)
    starts = jnp.arange(N // width, dtype=jnp.int32) * width
    kernel_t = epoch_kernel()

    def operate(direction):
        weighted = jnp.dot(kernel_t, observed * direction, precision=lax.Precision.HIGHEST, preferred_element_type=jnp.float32).astype(jnp.bfloat16)

        def block_product(start):
            block = lax.dynamic_slice_in_dim(scaled, start, width, 1)
            block_norm = lax.dynamic_slice_in_dim(sqnorm, start, width, 0)
            cross = jnp.dot(scaled.T, block, precision=lax.Precision.HIGHEST, preferred_element_type=jnp.float32)
            tile = jnp.exp(-0.5 * (sqnorm[:, None] + block_norm[None, :] - 2.0 * cross)).astype(jnp.bfloat16)
            return jnp.dot(weighted, tile, preferred_element_type=jnp.float32)
        spread = lax.map(block_product, starts)
        spread = jnp.transpose(spread, (1, 0, 2)).reshape(E, N)
        return observed * spread + noise_level * direction
    residual = observed * targets
    direction = residual
    solution = jnp.zeros((E, N), jnp.float32)
    norm_now = jnp.sum(residual * residual)
    for step in range(ITERS):
        image = operate(direction)
        alpha = norm_now / jnp.sum(direction * image)
        solution = solution + alpha * direction
        residual = residual - alpha * image
        norm_next = jnp.sum(residual * residual)
        direction = residual + norm_next / norm_now * direction
        norm_now = norm_next
    return (solution, residual)
```

```python
import functools
import math

import jax
import jax.numpy as jnp
from jax import lax
from jax.experimental import pallas as pl
from jax.experimental.pallas import tpu as pltpu
from jax.sharding import PartitionSpec as P

noise_level = 0.5
VMEM = pl.BlockSpec(memory_space=pltpu.VMEM)
bf16 = jnp.bfloat16
f32 = jnp.float32


def params(mib, **more):
    return pltpu.CompilerParams(vmem_limit_bytes=mib << 20, **more)


def epoch_kernel(epochs, total_count):
    s = lax.broadcasted_iota(jnp.int32, (epochs, epochs), 0)
    t = lax.broadcasted_iota(jnp.int32, (epochs, epochs), 1)
    gap = jnp.abs(s - t).astype(f32)
    return (8.0 / math.sqrt(total_count)) * jnp.exp(-gap / (epochs / 4.0))


def epoch_product(field, total_count):
    kernel_t = epoch_kernel(field.shape[0], total_count)
    return jnp.dot(
        kernel_t, field, precision=lax.Precision.HIGHEST, preferred_element_type=f32
    )


def prepare_kernel(total_count, feat_ref, scale_ref, target_ref, mask_ref, feats_ref, weighted_ref):
    scaled = feat_ref[...] / scale_ref[...] * math.sqrt(math.log2(math.e))
    high = scaled.astype(bf16)
    low = (scaled - high.astype(f32)).astype(bf16)
    count = scaled.shape[0]
    feats_ref[0:count, :] = high
    feats_ref[count:, :] = low
    start = target_ref[...] * mask_ref[...].astype(f32)
    weighted_ref[...] = epoch_product(start, total_count).astype(bf16)


def norm_parts(feats):
    count = feats.shape[0] // 2
    whole = feats[:count, :].astype(f32) + feats[count:, :].astype(f32)
    norm = -0.5 * jnp.sum(whole * whole, axis=0, keepdims=True)
    first = norm.astype(bf16).astype(f32)
    second = (norm - first).astype(bf16).astype(f32)
    third = norm - first - second
    return first, second, third


def block_kernel(
    step_rows, row_ref, col_ref, weighted_ref, tile_ref, part_ref, left, right, fields, total
):
    step = pl.program_id(0)
    width = row_ref.shape[2]
    count = row_ref.shape[1] // 2

    def rows(*parts):
        blank = jnp.zeros((16 - len(parts), width), f32)
        return jnp.concatenate(list(parts) + [blank], axis=0).astype(bf16)

    @pl.when(step == 0)
    def _():
        one = jnp.ones((1, width), f32)
        for block in range(row_ref.shape[0]):
            at = slice(block * width, (block + 1) * width)
            feats = row_ref[block]
            first, second, third = norm_parts(feats)
            right[0 : 2 * count, at] = feats
            right[2 * count : 4 * count, at] = feats
            right[4 * count :, at] = rows(one, one, one, first, second, third)
        for block in range(col_ref.shape[0]):
            at = slice(block * width, (block + 1) * width)
            feats = col_ref[block]
            first, second, third = norm_parts(feats)
            high = feats[0:count, :]
            low = feats[count:, :]
            left[0:count, at] = high
            left[count : 2 * count, at] = high
            left[2 * count : 3 * count, at] = low
            left[3 * count : 4 * count, at] = low
            left[4 * count :, at] = rows(first, second, third, one, one, one)
            fields[:, at] = weighted_ref[block]
        total[...] = jnp.zeros_like(total)

    at = pl.ds(pl.multiple_of(step * step_rows, step_rows), step_rows)
    power = lax.dot_general(
        left[:, at], right[...], (((0,), (0,)), ((), ())), preferred_element_type=f32
    )
    tile = jnp.exp2(power).astype(bf16)
    tile_ref[...] = tile
    total[...] += jnp.dot(fields[:, at], tile, preferred_element_type=f32)

    @pl.when(step == pl.num_programs(0) - 1)
    def _():
        for block in range(row_ref.shape[0]):
            at = slice(block * width, (block + 1) * width)
            part_ref[block] = total[:, at]


def middle_kernel(total_count, part_ref, target_ref, mask_ref, image_ref, weighted_ref, sums_ref):
    observed = mask_ref[...].astype(f32)
    start = target_ref[...] * observed
    spread = jnp.sum(part_ref[...].astype(f32), axis=0)
    image = observed * spread
    image_ref[...] = image
    weighted = epoch_product(image, total_count)
    high = weighted.astype(bf16).astype(f32)
    low = weighted - high
    weighted_ref[...] = jnp.concatenate([high, low], axis=0).T.astype(bf16)
    square = jnp.sum(start * start)
    cross = jnp.sum(start * image)
    lane = lax.broadcasted_iota(jnp.int32, sums_ref.shape, 1)
    sums_ref[...] = jnp.where(lane == 0, square, jnp.where(lane == 1, cross, 0.0))


def again_kernel(tile_ref, weighted_ref, part_ref):
    both = jnp.dot(tile_ref[...], weighted_ref[...], preferred_element_type=f32)
    epochs = both.shape[1] // 2
    flipped = both.T
    part_ref[0] = (flipped[:epochs] + flipped[epochs:]).astype(bf16)


def combine_kernel(
    sums_ref, part_ref, image_ref, target_ref, mask_ref, residual_ref, spread_ref, more_ref
):
    observed = mask_ref[...].astype(f32)
    start = target_ref[...] * observed
    image = image_ref[...]
    totals = jnp.sum(sums_ref[...], axis=0, keepdims=True)
    square, cross = totals[0:1, 0:1], totals[0:1, 1:2]
    alpha = square / (cross + noise_level * square)
    residual = start - alpha * (image + noise_level * start)
    second = observed * jnp.sum(part_ref[...].astype(f32), axis=0)
    spread = (1.0 - noise_level * alpha) * image - alpha * second
    residual_ref[...] = residual
    spread_ref[...] = spread
    lane = lax.broadcasted_iota(jnp.int32, more_ref.shape, 1)
    sums = (
        jnp.sum(residual * residual),
        jnp.sum(residual * spread),
        jnp.sum(residual * image),
    )
    row = jnp.zeros(more_ref.shape, f32)
    for place, value in enumerate(sums):
        row = jnp.where(lane == place, value, row)
    more_ref[...] = row


def finish_kernel(
    sums_ref, more_ref, residual_ref, spread_ref, image_ref, target_ref, mask_ref, sol_ref, res_ref
):
    observed = mask_ref[...].astype(f32)
    start = target_ref[...] * observed
    image = image_ref[...]
    residual = residual_ref[...]
    totals = jnp.sum(sums_ref[...], axis=0, keepdims=True)
    square, cross = totals[0:1, 0:1], totals[0:1, 1:2]
    alpha = square / (cross + noise_level * square)
    more = jnp.sum(more_ref[...], axis=0, keepdims=True)
    now, quad, mixed = more[0:1, 0:1], more[0:1, 1:2], more[0:1, 2:3]
    beta = now / square
    direction = residual + beta * start
    moved = spread_ref[...] + beta * image + noise_level * direction
    size = now + beta * beta * square + 2.0 * beta * (square - alpha * (cross + 0.5 * square))
    curve = quad + 2.0 * beta * mixed + beta * beta * cross + noise_level * size
    step = now / curve
    sol_ref[...] = alpha * start + step * direction
    res_ref[...] = residual - step * moved


def shards(features, lengthscale, targets, mask):
    rows, cols = lax.axis_size("row"), lax.axis_size("col")
    epochs, width = targets.shape
    feat = features.shape[0]
    total_count = width * rows * cols
    field = jax.ShapeDtypeStruct((epochs, width), f32)
    sums_shape = jax.ShapeDtypeStruct((1, 128), f32)

    feats, weighted = pl.pallas_call(
        functools.partial(prepare_kernel, total_count),
        out_shape=(
            jax.ShapeDtypeStruct((2 * feat, width), bf16),
            jax.ShapeDtypeStruct((epochs, width), bf16),
        ),
        in_specs=[VMEM] * 4,
        out_specs=[VMEM] * 2,
        compiler_params=params(8),
    )(features, lengthscale[:, None], targets, mask)

    spread_out = jnp.broadcast_to(weighted[None], (rows, epochs, width))
    col_weighted = lax.all_to_all(spread_out, "row", 0, 0)
    row_feats = lax.all_gather(feats, "col")
    col_feats = lax.all_gather(feats, "row")

    step_rows = 256
    depth = 4 * feat + 16
    tile, part = pl.pallas_call(
        functools.partial(block_kernel, step_rows),
        grid=(rows * width // step_rows,),
        out_shape=(
            jax.ShapeDtypeStruct((rows * width, cols * width), bf16),
            jax.ShapeDtypeStruct((cols, epochs, width), f32),
        ),
        in_specs=[VMEM] * 3,
        out_specs=[pl.BlockSpec((step_rows, cols * width), lambda s: (s, 0)), VMEM],
        scratch_shapes=[
            pltpu.VMEM((depth, rows * width), bf16),
            pltpu.VMEM((depth, cols * width), bf16),
            pltpu.VMEM((epochs, rows * width), bf16),
            pltpu.VMEM((epochs, cols * width), f32),
        ],
        compiler_params=params(40),
    )(row_feats, col_feats, col_weighted)

    pieces = lax.all_to_all(part, "col", 0, 0)
    image, weighted, sums = pl.pallas_call(
        functools.partial(middle_kernel, total_count),
        out_shape=(field, jax.ShapeDtypeStruct((width, 2 * epochs), bf16), sums_shape),
        in_specs=[VMEM] * 3,
        out_specs=[VMEM] * 3,
        compiler_params=params(8),
    )(pieces, targets, mask)

    devices = rows * cols
    sums = lax.all_to_all(
        jnp.broadcast_to(sums, (devices, 128)), ("row", "col"), 0, 0, tiled=True
    )
    row_weighted = lax.all_gather(weighted, "col", tiled=True)

    part = pl.pallas_call(
        again_kernel,
        grid=(rows,),
        out_shape=jax.ShapeDtypeStruct((rows, epochs, width), bf16),
        in_specs=[pl.BlockSpec((width, cols * width), lambda s: (s, 0)), VMEM],
        out_specs=pl.BlockSpec((1, epochs, width), lambda s: (s, 0, 0)),
        compiler_params=params(24),
    )(tile, row_weighted)

    pieces = lax.all_to_all(part, "row", 0, 0)
    residual, spread, more = pl.pallas_call(
        combine_kernel,
        out_shape=(field, field, sums_shape),
        in_specs=[VMEM] * 5,
        out_specs=[VMEM] * 3,
        compiler_params=params(8),
    )(sums, pieces, image, targets, mask)
    more = lax.all_to_all(
        jnp.broadcast_to(more, (devices, 128)), ("row", "col"), 0, 0, tiled=True
    )
    return pl.pallas_call(
        finish_kernel,
        out_shape=(field, field),
        in_specs=[VMEM] * 7,
        out_specs=[VMEM] * 2,
        compiler_params=params(8),
    )(sums, more, residual, spread, image, targets, mask)


def solution(mesh):
    whole = P(None, ("row", "col"))
    return jax.shard_map(
        shards,
        mesh=mesh,
        in_specs=(whole, P(), whole, whole),
        out_specs=(whole, whole),
        check_vma=False,
    )
```

```python
import functools
import math

import jax
import jax.numpy as jnp
from jax import lax
from jax.experimental import pallas as pl
from jax.experimental.pallas import tpu as pltpu
from jax.sharding import PartitionSpec as P

noise_level = 0.5
VMEM = pl.BlockSpec(memory_space=pltpu.VMEM)
bf16 = jnp.bfloat16
f32 = jnp.float32


def params(mib, **more):
    return pltpu.CompilerParams(vmem_limit_bytes=mib << 20, **more)


def epoch_kernel(epochs, total_count):
    s = lax.broadcasted_iota(jnp.int32, (epochs, epochs), 0)
    t = lax.broadcasted_iota(jnp.int32, (epochs, epochs), 1)
    gap = jnp.abs(s - t).astype(f32)
    return (8.0 / math.sqrt(total_count)) * jnp.exp(-gap / (epochs / 4.0))


def epoch_product(field, total_count):
    kernel_t = epoch_kernel(field.shape[0], total_count)
    return jnp.dot(
        kernel_t, field, precision=lax.Precision.HIGHEST, preferred_element_type=f32
    )


def prepare_kernel(total_count, feat_ref, scale_ref, target_ref, mask_ref, feats_ref, out_ref, pack, sem):
    scaled = feat_ref[...] / scale_ref[...] * math.sqrt(math.log2(math.e))
    high = scaled.astype(bf16)
    low = (scaled - high.astype(f32)).astype(bf16)
    count = scaled.shape[0]
    feats_ref[0:count, :] = high
    feats_ref[count:, :] = low
    pack[0:count, :] = high
    pack[count : 2 * count, :] = low
    start = target_ref[...] * mask_ref[...].astype(f32)
    pack[2 * count :, :] = epoch_product(start, total_count).astype(bf16)
    send_all(pack, out_ref, sem)


def send_all(source, out_ref, sem):
    copies = [
        pltpu.make_async_copy(source, out_ref.at[place], sem.at[place])
        for place in range(out_ref.shape[0])
    ]
    for copy in copies:
        copy.start()
    for copy in copies:
        copy.wait()


def norm_parts(feats):
    count = feats.shape[0] // 2
    whole = feats[:count, :].astype(f32) + feats[count:, :].astype(f32)
    norm = -0.5 * jnp.sum(whole * whole, axis=0, keepdims=True)
    first = norm.astype(bf16).astype(f32)
    second = (norm - first).astype(bf16).astype(f32)
    third = norm - first - second
    return first, second, third


def block_kernel(step_rows, row_ref, col_ref, tile_ref, part_ref, left, right, fields):
    step = pl.program_id(0)
    blocks, epochs, width = part_ref.shape
    count = row_ref.shape[1] // 2
    total = part_ref

    def rows(*parts):
        blank = jnp.zeros((16 - len(parts), width), f32)
        return jnp.concatenate(list(parts) + [blank], axis=0).astype(bf16)

    @pl.when(step == 0)
    def _():
        one = jnp.ones((1, width), f32)
        for block in range(row_ref.shape[0]):
            at = slice(block * width, (block + 1) * width)
            feats = row_ref[block]
            first, second, third = norm_parts(feats)
            right[0 : 2 * count, at] = feats
            right[2 * count : 4 * count, at] = feats
            right[4 * count :, at] = rows(one, one, one, first, second, third)
        for block in range(col_ref.shape[0]):
            at = slice(block * width, (block + 1) * width)
            feats = col_ref[block, 0 : 2 * count, :]
            first, second, third = norm_parts(feats)
            high = feats[0:count, :]
            low = feats[count:, :]
            left[0:count, at] = high
            left[count : 2 * count, at] = high
            left[2 * count : 3 * count, at] = low
            left[3 * count : 4 * count, at] = low
            left[4 * count :, at] = rows(first, second, third, one, one, one)
            fields[:, at] = col_ref[block, 2 * count :, :]
        part_ref[...] = jnp.zeros_like(part_ref)

    at = pl.ds(pl.multiple_of(step * step_rows, step_rows), step_rows)
    power = lax.dot_general(
        left[:, at], right[...], (((0,), (0,)), ((), ())), preferred_element_type=f32
    )
    tile = jnp.exp2(power).astype(bf16)
    tile_ref[...] = tile
    spread = jnp.dot(fields[:, at], tile, preferred_element_type=f32)
    for block in range(blocks):
        part_ref[block] += spread[:, block * width : (block + 1) * width]


def middle_kernel(
    total_count, part_ref, target_ref, mask_ref, image_ref, out_ref, sums_ref, pack, sem
):
    observed = mask_ref[...].astype(f32)
    start = target_ref[...] * observed
    image = observed * jnp.sum(part_ref[...], axis=0)
    image_ref[...] = image
    pack[...] = epoch_product(image, total_count).astype(bf16)
    send_all(pack, out_ref, sem)
    sums_ref[...] = lanes(
        jnp.sum(start * start), jnp.sum(start * image), jnp.sum(image * image)
    )


def lanes(*values):
    lane = lax.broadcasted_iota(jnp.int32, (1, 128), 1)
    row = jnp.zeros((1, 128), f32)
    for place, value in enumerate(values):
        row = jnp.where(lane == place, value, row)
    return row


def again_kernel(step_rows, tile_ref, col_ref, part_ref, held, fields, sem):
    blocks, epochs, width = part_ref.shape
    steps = held.shape[0] // step_rows

    def load(step):
        at = pl.ds(pl.multiple_of(step * step_rows, step_rows), step_rows)
        return pltpu.make_async_copy(tile_ref.at[at], held.at[at], sem.at[step])

    for step in range(steps):
        load(step).start()
    for block in range(col_ref.shape[0]):
        fields[:, block * width : (block + 1) * width] = col_ref[block]
    part_ref[...] = jnp.zeros_like(part_ref)

    def body(step, carry):
        load(step).wait()
        at = pl.ds(pl.multiple_of(step * step_rows, step_rows), step_rows)
        spread = jnp.dot(fields[:, at], held[at, :], preferred_element_type=f32)
        for block in range(blocks):
            part_ref[block] += spread[:, block * width : (block + 1) * width]
        return carry

    lax.fori_loop(0, steps, body, 0)


def last_kernel(part_ref, image_ref, target_ref, mask_ref, sums_ref, second_ref, out_ref):
    observed = mask_ref[...].astype(f32)
    second = observed * jnp.sum(part_ref[...], axis=0)
    second_ref[...] = second
    row = sums_ref[...] + lanes(0.0, 0.0, 0.0, jnp.sum(image_ref[...] * second))
    out_ref[...] = jnp.broadcast_to(row, out_ref.shape)


def finish_kernel(
    sums_ref, image_ref, second_ref, target_ref, mask_ref, sol_ref, res_ref
):
    start = target_ref[...] * mask_ref[...].astype(f32)
    image = image_ref[...]
    totals = jnp.sum(sums_ref[...], axis=0, keepdims=True)
    b00, b01 = totals[:, 0:1], totals[:, 1:2]
    b11, b12 = totals[:, 2:3], totals[:, 3:4]
    mean = b01 / b00
    alpha = 1.0 / (mean + noise_level)
    residual = alpha * (mean * start - image)
    now = alpha * alpha * (b11 - mean * b01)
    beta = now / b00
    direction = residual + beta * start
    moved = (alpha * mean + beta) * image - alpha * second_ref[...] + noise_level * direction
    quad = alpha * alpha * (b12 - 2.0 * mean * b11 + mean * mean * b01)
    mixed = alpha * (mean * b01 - b11)
    curve = quad + 2.0 * beta * mixed + beta * beta * b01
    curve = curve + noise_level * (now + beta * beta * b00)
    step = now / curve
    sol_ref[...] = alpha * start + step * direction
    res_ref[...] = residual - step * moved


def shards(features, lengthscale, targets, mask):
    rows, cols = lax.axis_size("row"), lax.axis_size("col")
    devices = rows * cols
    epochs, width = targets.shape
    feat = features.shape[0]
    total_count = width * devices
    field = jax.ShapeDtypeStruct((epochs, width), f32)
    sums_shape = jax.ShapeDtypeStruct((1, 128), f32)
    part_shape = jax.ShapeDtypeStruct((cols, epochs, width), f32)
    away = pl.BlockSpec(memory_space=pl.ANY)
    pack_rows = 2 * feat + epochs

    feats, pack = pl.pallas_call(
        functools.partial(prepare_kernel, total_count),
        out_shape=(
            jax.ShapeDtypeStruct((2 * feat, width), bf16),
            jax.ShapeDtypeStruct((rows, pack_rows, width), bf16),
        ),
        in_specs=[VMEM] * 4,
        out_specs=[VMEM, away],
        scratch_shapes=[
            pltpu.VMEM((pack_rows, width), bf16),
            pltpu.SemaphoreType.DMA((rows,)),
        ],
        compiler_params=params(8),
    )(features, lengthscale[:, None], targets, mask)

    col_pack = lax.all_to_all(pack, "row", 0, 0)
    row_feats = lax.all_gather(feats, "col")

    step_rows = 768
    depth = 4 * feat + 16
    tile, part = pl.pallas_call(
        functools.partial(block_kernel, step_rows),
        grid=(rows * width // step_rows,),
        out_shape=(jax.ShapeDtypeStruct((rows * width, cols * width), bf16), part_shape),
        in_specs=[VMEM] * 2,
        out_specs=[pl.BlockSpec((step_rows, cols * width), lambda s: (s, 0)), VMEM],
        scratch_shapes=[
            pltpu.VMEM((depth, rows * width), bf16),
            pltpu.VMEM((depth, cols * width), bf16),
            pltpu.VMEM((epochs, rows * width), bf16),
        ],
        compiler_params=params(48),
    )(row_feats, col_pack)

    pieces = lax.all_to_all(part, "col", 0, 0)
    image, pack, sums = pl.pallas_call(
        functools.partial(middle_kernel, total_count),
        out_shape=(field, jax.ShapeDtypeStruct((rows, epochs, width), bf16), sums_shape),
        in_specs=[VMEM] * 3,
        out_specs=[VMEM, away, VMEM],
        scratch_shapes=[
            pltpu.VMEM((epochs, width), bf16),
            pltpu.SemaphoreType.DMA((rows,)),
        ],
        compiler_params=params(8),
    )(pieces, targets, mask)
    col_weighted = lax.all_to_all(pack, "row", 0, 0)

    again_rows = 512
    part = pl.pallas_call(
        functools.partial(again_kernel, again_rows),
        out_shape=part_shape,
        in_specs=[away, VMEM],
        out_specs=VMEM,
        scratch_shapes=[
            pltpu.VMEM((rows * width, cols * width), bf16),
            pltpu.VMEM((epochs, rows * width), bf16),
            pltpu.SemaphoreType.DMA((rows * width // again_rows,)),
        ],
        compiler_params=params(50),
    )(tile, col_weighted)

    pieces = lax.all_to_all(part, "col", 0, 0)
    second, sums = pl.pallas_call(
        last_kernel,
        out_shape=(field, jax.ShapeDtypeStruct((devices, 128), f32)),
        in_specs=[VMEM] * 5,
        out_specs=[VMEM] * 2,
        compiler_params=params(8),
    )(pieces, image, targets, mask, sums)
    sums = lax.all_to_all(sums, ("row", "col"), 0, 0, tiled=True)
    return pl.pallas_call(
        finish_kernel,
        out_shape=(field, field),
        in_specs=[VMEM] * 5,
        out_specs=[VMEM] * 2,
        compiler_params=params(8),
    )(sums, image, second, targets, mask)


def solution(mesh):
    whole = P(None, ("row", "col"))
    return jax.shard_map(
        shards,
        mesh=mesh,
        in_specs=(whole, P(), whole, whole),
        out_specs=(whole, whole),
        check_vma=False,
    )
```

```python
import functools
import math

import jax
import jax.numpy as jnp
from jax import lax
from jax.experimental import pallas as pl
from jax.experimental.pallas import tpu as pltpu
from jax.sharding import PartitionSpec as P

noise_level = 0.5
VMEM = pl.BlockSpec(memory_space=pltpu.VMEM)
bf16 = jnp.bfloat16
f32 = jnp.float32


def params(mib, **more):
    return pltpu.CompilerParams(vmem_limit_bytes=mib << 20, **more)


def epoch_kernel(epochs, total_count):
    s = lax.broadcasted_iota(jnp.int32, (epochs, epochs), 0)
    t = lax.broadcasted_iota(jnp.int32, (epochs, epochs), 1)
    gap = jnp.abs(s - t).astype(f32)
    return (8.0 / math.sqrt(total_count)) * jnp.exp(-gap / (epochs / 4.0))


def epoch_product(field, total_count):
    kernel_t = epoch_kernel(field.shape[0], total_count)
    return jnp.dot(
        kernel_t, field, precision=lax.Precision.HIGHEST, preferred_element_type=f32
    )


def prepare_kernel(
    total_count, feat_in, scale_ref, target_in, mask_in, feats_ref, out_ref,
    feat_ref, target_ref, mask_ref, pack, sem, load_sem,
):
    loads = [
        pltpu.make_async_copy(source, target, load_sem.at[place])
        for place, (source, target) in enumerate(
            ((feat_in, feat_ref), (target_in, target_ref), (mask_in, mask_ref))
        )
    ]
    for load in loads:
        load.start()
    count = feat_ref.shape[0]
    across = lax.broadcasted_iota(jnp.int32, (count, count), 0)
    down = lax.broadcasted_iota(jnp.int32, (count, count), 1)
    scale = jnp.sum(jnp.where(across == down, scale_ref[...], 0.0), axis=1, keepdims=True)
    loads[0].wait()
    scaled = feat_ref[...] / scale * math.sqrt(math.log2(math.e))
    high = scaled.astype(bf16)
    low = (scaled - high.astype(f32)).astype(bf16)
    feats_ref[0:count, :] = high
    feats_ref[count:, :] = low
    pack[0:count, :] = high
    pack[count : 2 * count, :] = low
    loads[1].wait()
    loads[2].wait()
    start = target_ref[...] * mask_ref[...].astype(f32)
    pack[2 * count :, :] = epoch_product(start, total_count).astype(bf16)
    send_all(pack, out_ref, sem)


def send_all(source, out_ref, sem):
    copies = [
        pltpu.make_async_copy(source, out_ref.at[place], sem.at[place])
        for place in range(out_ref.shape[0])
    ]
    for copy in copies:
        copy.start()
    for copy in copies:
        copy.wait()


def norm_parts(feats):
    count = feats.shape[0] // 2
    whole = feats[:count, :].astype(f32) + feats[count:, :].astype(f32)
    norm = -0.5 * jnp.sum(whole * whole, axis=0, keepdims=True)
    first = norm.astype(bf16).astype(f32)
    second = (norm - first).astype(bf16).astype(f32)
    third = norm - first - second
    return first, second, third


def block_kernel(
    step_rows, row_ref, col_ref, tile_ref, mine_ref, other_ref, left, right, fields, part_ref
):
    step = pl.program_id(0)
    blocks, epochs, width = part_ref.shape
    count = row_ref.shape[1] // 2
    total = part_ref

    def rows(*parts):
        blank = jnp.zeros((16 - len(parts), width), f32)
        return jnp.concatenate(list(parts) + [blank], axis=0).astype(bf16)

    @pl.when(step == 0)
    def _():
        one = jnp.ones((1, width), f32)
        for block in range(row_ref.shape[0]):
            at = slice(block * width, (block + 1) * width)
            feats = row_ref[block]
            first, second, third = norm_parts(feats)
            right[0 : 2 * count, at] = feats
            right[2 * count : 4 * count, at] = feats
            right[4 * count :, at] = rows(one, one, one, first, second, third)
        for block in range(col_ref.shape[0]):
            at = slice(block * width, (block + 1) * width)
            feats = col_ref[block, 0 : 2 * count, :]
            first, second, third = norm_parts(feats)
            high = feats[0:count, :]
            low = feats[count:, :]
            left[0:count, at] = high
            left[count : 2 * count, at] = high
            left[2 * count : 3 * count, at] = low
            left[3 * count : 4 * count, at] = low
            left[4 * count :, at] = rows(first, second, third, one, one, one)
            fields[:, at] = col_ref[block, 2 * count :, :]
        part_ref[...] = jnp.zeros_like(part_ref)

    at = pl.ds(pl.multiple_of(step * step_rows, step_rows), step_rows)
    power = lax.dot_general(
        left[:, at], right[...], (((0,), (0,)), ((), ())), preferred_element_type=f32
    )
    tile = jnp.exp2(power).astype(bf16)
    tile_ref[...] = tile
    spread = jnp.dot(fields[:, at], tile, preferred_element_type=f32)
    for block in range(blocks):
        part_ref[block] += spread[:, block * width : (block + 1) * width]

    @pl.when(step == pl.num_programs(0) - 1)
    def _():
        split_parts(part_ref, mine_ref, other_ref)


def split_parts(part_ref, mine_ref, other_ref):
    core = lax.rem(lax.axis_index("col"), 2)
    for place in range(mine_ref.shape[0]):
        mine_ref[place] = part_ref[2 * place + core]
        other_ref[place] = part_ref[2 * place + 1 - core]


def add_kernel(mine_ref, other_ref, *out_refs):
    count = mine_ref.shape[0]
    here = lax.axis_index("col") // 2
    for shift, out_ref in enumerate(out_refs):
        place = lax.rem(here + shift, count)
        out_ref[...] = mine_ref[place] + other_ref[place]


def scatter_sum(mine, other):
    count = mine.shape[0]
    cols = 2 * count
    other = lax.ppermute(other, "col", [(k, k ^ 1) for k in range(cols)])
    block = jax.ShapeDtypeStruct(mine.shape[1:], f32)
    terms = pl.pallas_call(
        add_kernel,
        out_shape=(block,) * count,
        in_specs=[VMEM] * 2,
        out_specs=[VMEM] * count,
        compiler_params=params(8),
    )(mine, other)
    return [
        lax.ppermute(term, "col", [(k, (k + 2 * shift) % cols) for k in range(cols)])
        if shift
        else term
        for shift, term in enumerate(terms)
    ]


def middle_kernel(
    total_count, *refs
):
    *part_refs, target_ref, mask_ref, image_ref, out_ref, sums_ref, pack, sem = refs
    observed = mask_ref[...].astype(f32)
    start = target_ref[...] * observed
    image = observed * sum(part_ref[...] for part_ref in part_refs)
    image_ref[...] = image
    pack[...] = epoch_product(image, total_count).astype(bf16)
    send_all(pack, out_ref, sem)
    sums_ref[...] = lanes(
        jnp.sum(start * start), jnp.sum(start * image), jnp.sum(image * image)
    )


def lanes(*values):
    lane = lax.broadcasted_iota(jnp.int32, (1, 128), 1)
    row = jnp.zeros((1, 128), f32)
    for place, value in enumerate(values):
        row = jnp.where(lane == place, value, row)
    return row


def again_kernel(
    step_rows, tile_ref, col_ref, image_ref, sums_ref, mine_ref, other_ref, out_ref,
    held, fields, part_ref, sem,
):
    blocks, epochs, width = part_ref.shape
    steps = held.shape[0] // step_rows

    def load(step):
        at = pl.ds(pl.multiple_of(step * step_rows, step_rows), step_rows)
        return pltpu.make_async_copy(tile_ref.at[at], held.at[at], sem.at[step])

    for step in range(steps):
        load(step).start()
    for block in range(col_ref.shape[0]):
        fields[:, block * width : (block + 1) * width] = col_ref[block]
    part_ref[...] = jnp.zeros_like(part_ref)

    def body(step, carry):
        load(step).wait()
        at = pl.ds(pl.multiple_of(step * step_rows, step_rows), step_rows)
        spread = jnp.dot(fields[:, at], held[at, :], preferred_element_type=f32)
        for block in range(blocks):
            part_ref[block] += spread[:, block * width : (block + 1) * width]
        return carry

    lax.fori_loop(0, steps, body, 0)
    split_parts(part_ref, mine_ref, other_ref)
    cross = jnp.zeros((epochs, width), f32)
    for block in range(blocks):
        cross = cross + part_ref[block] * image_ref[block]
    row = sums_ref[...] + lanes(0.0, 0.0, 0.0, jnp.sum(cross))
    out_ref[...] = jnp.broadcast_to(row, out_ref.shape)


def finish_kernel(*refs):
    *part_refs, sums_ref, image_ref, target_ref, mask_ref, sol_ref, res_ref = refs
    observed = mask_ref[...].astype(f32)
    start = target_ref[...] * observed
    image = image_ref[...]
    second = observed * sum(part_ref[...] for part_ref in part_refs)
    totals = jnp.sum(sums_ref[...], axis=0, keepdims=True)
    b00, b01 = totals[:, 0:1], totals[:, 1:2]
    b11, b12 = totals[:, 2:3], totals[:, 3:4]
    mean = b01 / b00
    alpha = 1.0 / (mean + noise_level)
    residual = alpha * (mean * start - image)
    now = alpha * alpha * (b11 - mean * b01)
    beta = now / b00
    direction = residual + beta * start
    moved = (alpha * mean + beta) * image - alpha * second + noise_level * direction
    quad = alpha * alpha * (b12 - 2.0 * mean * b11 + mean * mean * b01)
    mixed = alpha * (mean * b01 - b11)
    curve = quad + 2.0 * beta * mixed + beta * beta * b01
    curve = curve + noise_level * (now + beta * beta * b00)
    step = now / curve
    sol_ref[...] = alpha * start + step * direction
    res_ref[...] = residual - step * moved


def shards(features, lengthscale, targets, mask):
    rows, cols = lax.axis_size("row"), lax.axis_size("col")
    devices = rows * cols
    epochs, width = targets.shape
    feat = features.shape[0]
    total_count = width * devices
    field = jax.ShapeDtypeStruct((epochs, width), f32)
    sums_shape = jax.ShapeDtypeStruct((1, 128), f32)
    half_shape = jax.ShapeDtypeStruct((cols // 2, epochs, width), f32)
    part_scratch = pltpu.VMEM((cols, epochs, width), f32)
    away = pl.BlockSpec(memory_space=pl.ANY)
    hbm = pl.BlockSpec(memory_space=pltpu.HBM)
    pack_rows = 2 * feat + epochs

    feats, pack = pl.pallas_call(
        functools.partial(prepare_kernel, total_count),
        out_shape=(
            jax.ShapeDtypeStruct((2 * feat, width), bf16),
            jax.ShapeDtypeStruct((rows, pack_rows, width), bf16),
        ),
        in_specs=[hbm, VMEM, hbm, hbm],
        out_specs=[VMEM, away],
        scratch_shapes=[
            pltpu.VMEM((feat, width), f32),
            pltpu.VMEM((epochs, width), f32),
            pltpu.VMEM((epochs, width), jnp.int32),
            pltpu.VMEM((pack_rows, width), bf16),
            pltpu.SemaphoreType.DMA((rows,)),
            pltpu.SemaphoreType.DMA((3,)),
        ],
        compiler_params=params(60),
    )(features, lengthscale[None, :], targets, mask)

    col_pack = lax.all_to_all(pack, "row", 0, 0)
    row_feats = lax.all_gather(feats, "col")

    step_rows = 768
    depth = 4 * feat + 16
    tile, mine, other = pl.pallas_call(
        functools.partial(block_kernel, step_rows),
        grid=(rows * width // step_rows,),
        out_shape=(
            jax.ShapeDtypeStruct((rows * width, cols * width), bf16),
            half_shape,
            half_shape,
        ),
        in_specs=[VMEM] * 2,
        out_specs=[pl.BlockSpec((step_rows, cols * width), lambda s: (s, 0)), VMEM, VMEM],
        scratch_shapes=[
            pltpu.VMEM((depth, rows * width), bf16),
            pltpu.VMEM((depth, cols * width), bf16),
            pltpu.VMEM((epochs, rows * width), bf16),
            part_scratch,
        ],
        compiler_params=params(48),
    )(row_feats, col_pack)

    terms = scatter_sum(mine, other)
    image, pack, sums = pl.pallas_call(
        functools.partial(middle_kernel, total_count),
        out_shape=(field, jax.ShapeDtypeStruct((rows, epochs, width), bf16), sums_shape),
        in_specs=[VMEM] * (len(terms) + 2),
        out_specs=[VMEM, away, VMEM],
        scratch_shapes=[
            pltpu.VMEM((epochs, width), bf16),
            pltpu.SemaphoreType.DMA((rows,)),
        ],
        compiler_params=params(8),
    )(*terms, targets, mask)
    col_weighted = lax.all_to_all(pack, "row", 0, 0)
    row_images = lax.all_gather(image, "col")

    again_rows = 512
    mine, other, sums = pl.pallas_call(
        functools.partial(again_kernel, again_rows),
        out_shape=(half_shape, half_shape, jax.ShapeDtypeStruct((devices, 128), f32)),
        in_specs=[away, VMEM, VMEM, VMEM],
        out_specs=[VMEM] * 3,
        scratch_shapes=[
            pltpu.VMEM((rows * width, cols * width), bf16),
            pltpu.VMEM((epochs, rows * width), bf16),
            part_scratch,
            pltpu.SemaphoreType.DMA((rows * width // again_rows,)),
        ],
        compiler_params=params(50),
    )(tile, col_weighted, row_images, sums)

    sums = lax.all_to_all(sums, ("row", "col"), 0, 0, tiled=True)
    terms = scatter_sum(mine, other)
    return pl.pallas_call(
        finish_kernel,
        out_shape=(field, field),
        in_specs=[VMEM] * (len(terms) + 4),
        out_specs=[VMEM] * 2,
        compiler_params=params(8),
    )(*terms, sums, image, targets, mask)


def solution(mesh):
    whole = P(None, ("row", "col"))
    return jax.shard_map(
        shards,
        mesh=mesh,
        in_specs=(whole, P(), whole, whole),
        out_specs=(whole, whole),
        check_vma=False,
    )
```

```python
import functools
import math

import jax
import jax.numpy as jnp
from jax import lax
from jax.experimental import pallas as pl
from jax.experimental.pallas import tpu as pltpu
from jax.sharding import PartitionSpec as P

noise_level = 0.5
AGAIN = 2
FAT = 8
COL = ("y", "core")
VMEM = pl.BlockSpec(memory_space=pltpu.VMEM)
bf16 = jnp.bfloat16
f32 = jnp.float32


def params(mib, **more):
    return pltpu.CompilerParams(vmem_limit_bytes=mib << 20, **more)


def epoch_kernel(epochs, total_count):
    s = lax.broadcasted_iota(jnp.int32, (epochs, epochs), 0)
    t = lax.broadcasted_iota(jnp.int32, (epochs, epochs), 1)
    gap = jnp.abs(s - t).astype(f32)
    return (8.0 / math.sqrt(total_count)) * jnp.exp(-gap / (epochs / 4.0))


def epoch_product(field, total_count):
    kernel_t = epoch_kernel(field.shape[0], total_count)
    return jnp.dot(
        kernel_t, field, precision=lax.Precision.HIGHEST, preferred_element_type=f32
    )


def prepare_kernel(
    total_count, feat_in, scale_ref, target_in, mask_in, feats_ref, out_ref,
    feat_ref, target_ref, mask_ref, pack, sem, load_sem,
):
    loads = [
        pltpu.make_async_copy(source, target, load_sem.at[place])
        for place, (source, target) in enumerate(
            ((feat_in, feat_ref), (target_in, target_ref), (mask_in, mask_ref))
        )
    ]
    for load in loads:
        load.start()
    count = feat_ref.shape[0]
    across = lax.broadcasted_iota(jnp.int32, (count, count), 0)
    down = lax.broadcasted_iota(jnp.int32, (count, count), 1)
    scale = jnp.sum(jnp.where(across == down, scale_ref[...], 0.0), axis=1, keepdims=True)
    loads[0].wait()
    scaled = feat_ref[...] / scale * math.sqrt(math.log2(math.e))
    high = scaled.astype(bf16)
    low = (scaled - high.astype(f32)).astype(bf16)
    feats_ref[0:count, :] = high
    feats_ref[count:, :] = low
    pack[0:count, :] = high
    pack[count : 2 * count, :] = low
    loads[1].wait()
    loads[2].wait()
    start = target_ref[...] * mask_ref[...].astype(f32)
    pack[2 * count :, :] = epoch_product(start, total_count).astype(bf16)
    send_all(pack, out_ref, sem)


def send_all(source, out_ref, sem):
    copies = [
        pltpu.make_async_copy(source, out_ref.at[place], sem.at[place])
        for place in range(out_ref.shape[0])
    ]
    for copy in copies:
        copy.start()
    for copy in copies:
        copy.wait()


def norm_parts(feats):
    count = feats.shape[0] // 2
    whole = feats[:count, :].astype(f32) + feats[count:, :].astype(f32)
    norm = -0.5 * jnp.sum(whole * whole, axis=0, keepdims=True)
    first = norm.astype(bf16).astype(f32)
    second = (norm - first).astype(bf16).astype(f32)
    third = norm - first - second
    return first, second, third


def block_kernel(
    step_rows, row_ref, col_ref, tile_ref, right, tail_ref, mine_ref, other_ref,
    left, fields, part_ref,
):
    step = pl.program_id(0)
    blocks, epochs, width = part_ref.shape
    count = row_ref.shape[1] // 2
    total = part_ref

    def rows(*parts):
        blank = jnp.zeros((16 - len(parts), width), f32)
        return jnp.concatenate(list(parts) + [blank], axis=0).astype(bf16)

    @pl.when(step == 0)
    def _():
        one = jnp.ones((1, width), f32)
        for block in range(row_ref.shape[0]):
            at = slice(block * width, (block + 1) * width)
            feats = row_ref[block]
            first, second, third = norm_parts(feats)
            right[0 : 2 * count, at] = feats
            right[2 * count : 4 * count, at] = feats
            right[4 * count :, at] = rows(one, one, one, first, second, third)
        for block in range(col_ref.shape[0]):
            at = slice(block * width, (block + 1) * width)
            feats = col_ref[block, 0 : 2 * count, :]
            first, second, third = norm_parts(feats)
            high = feats[0:count, :]
            low = feats[count:, :]
            left[0:count, at] = high
            left[count : 2 * count, at] = high
            left[2 * count : 3 * count, at] = low
            left[3 * count : 4 * count, at] = low
            left[4 * count :, at] = rows(first, second, third, one, one, one)
            fields[:, at] = col_ref[block, 2 * count :, :]
        part_ref[...] = jnp.zeros_like(part_ref)
        tail_ref[...] = left[:, left.shape[1] - tail_ref.shape[1] :]

    at = pl.ds(pl.multiple_of(step * step_rows, step_rows), step_rows)
    power = lax.dot_general(
        left[:, at], right[...], (((0,), (0,)), ((), ())), preferred_element_type=f32
    )
    tile = jnp.exp2(power).astype(bf16)
    tile_ref[...] = tile
    spread = jnp.dot(fields[:, at], tile, preferred_element_type=f32)
    for block in range(blocks):
        part_ref[block] += spread[:, block * width : (block + 1) * width]

    @pl.when(step == pl.num_programs(0) - 1)
    def _():
        split_parts(part_ref, mine_ref, other_ref)


def split_parts(part_ref, mine_ref, other_ref):
    core = lax.axis_index("core")
    epochs = part_ref.shape[1]
    for place in range(mine_ref.shape[0]):
        mine_ref[place, 0:epochs, :] = part_ref[2 * place + core]
        other_ref[place, 0:epochs, :] = part_ref[2 * place + 1 - core]


def add_kernel(mine_ref, other_ref, *out_refs):
    count = mine_ref.shape[0]
    epochs = out_refs[0].shape[0]
    here = lax.axis_index("y")
    for shift, out_ref in enumerate(out_refs[:count]):
        place = lax.rem(here + shift, count)
        out_ref[...] = mine_ref[place, 0:epochs, :] + other_ref[place, 0:epochs, :]
    for sums_ref in out_refs[count:]:
        row = mine_ref[0, epochs:, 0:128] + other_ref[0, epochs:, 0:128]
        sums_ref[...] = jnp.broadcast_to(row[None], sums_ref.shape)


def pair_sum(mine, other, block, *more):
    count = mine.shape[0]
    other = lax.ppermute(other, "core", [(0, 1), (1, 0)])
    return pl.pallas_call(
        add_kernel,
        out_shape=(block,) * count + more,
        in_specs=[VMEM] * 2,
        out_specs=[VMEM] * (count + len(more)),
        compiler_params=params(8),
    )(mine, other)


def exchange(terms):
    count = len(terms)
    return [
        lax.ppermute(term, "y", [(k, (k + shift) % count) for k in range(count)])
        if shift
        else term
        for shift, term in enumerate(terms)
    ]


def middle_kernel(
    total_count, *refs
):
    *part_refs, target_ref, mask_ref, image_ref, out_ref, sums_ref, pack, sem = refs
    observed = mask_ref[...].astype(f32)
    start = target_ref[...] * observed
    image = observed * sum(part_ref[...] for part_ref in part_refs)
    image_ref[...] = image
    pack[...] = epoch_product(image, total_count).astype(bf16)
    send_all(pack, out_ref, sem)
    sums_ref[...] = lanes(
        jnp.sum(start * start), jnp.sum(start * image), jnp.sum(image * image)
    )


def lanes(*values):
    lane = lax.broadcasted_iota(jnp.int32, (1, 128), 1)
    row = jnp.zeros((1, 128), f32)
    for place, value in enumerate(values):
        row = jnp.where(lane == place, value, row)
    return row


def again_kernel(
    step_rows, tile_ref, right_ref, left_ref, col_ref, image_ref, sums_ref, mine_ref, other_ref,
    held, fields, part_ref, sem,
):
    blocks, epochs, width = part_ref.shape
    steps = held.shape[0] // step_rows

    def load(step):
        at = pl.ds(pl.multiple_of(step * step_rows, step_rows), step_rows)
        return pltpu.make_async_copy(tile_ref.at[at], held.at[at], sem.at[step])

    for step in range(steps):
        load(step).start()
    for block in range(col_ref.shape[0]):
        fields[:, block * width : (block + 1) * width] = col_ref[block]
    part_ref[...] = jnp.zeros_like(part_ref)

    def add(at, tile):
        spread = jnp.dot(fields[:, at], tile, preferred_element_type=f32)
        for block in range(blocks):
            part_ref[block] += spread[:, block * width : (block + 1) * width]

    def again(step, carry):
        at = pl.ds(pl.multiple_of(step * step_rows, step_rows), step_rows)
        power = lax.dot_general(
            left_ref[:, at], right_ref[...], (((0,), (0,)), ((), ())), preferred_element_type=f32
        )
        at = pl.ds(pl.multiple_of(held.shape[0] + step * step_rows, step_rows), step_rows)
        add(at, jnp.exp2(power).astype(bf16))
        return carry

    def body(step, carry):
        load(step).wait()
        at = pl.ds(pl.multiple_of(step * step_rows, step_rows), step_rows)
        add(at, held[at, :])
        return carry

    lax.fori_loop(0, left_ref.shape[1] // step_rows, again, 0)

    lax.fori_loop(0, steps, body, 0)
    split_parts(part_ref, mine_ref, other_ref)
    cross = jnp.zeros((epochs, width), f32)
    for block in range(blocks):
        cross = cross + part_ref[block] * image_ref[block]
    row = sums_ref[...] + lanes(0.0, 0.0, 0.0, jnp.sum(cross))
    for half_ref in (mine_ref, other_ref):
        half_ref[0, epochs:, 0:128] = jnp.broadcast_to(row, (8, 128))


def finish_kernel(*refs):
    *part_refs, sums_ref, image_ref, target_ref, mask_ref, sol_ref, res_ref = refs
    observed = mask_ref[...].astype(f32)
    start = target_ref[...] * observed
    image = image_ref[...]
    second = observed * sum(part_ref[...] for part_ref in part_refs)
    totals = jnp.sum(sums_ref[...], axis=0)[0:1]
    b00, b01 = totals[:, 0:1], totals[:, 1:2]
    b11, b12 = totals[:, 2:3], totals[:, 3:4]
    mean = b01 / b00
    alpha = 1.0 / (mean + noise_level)
    residual = alpha * (mean * start - image)
    now = alpha * alpha * (b11 - mean * b01)
    beta = now / b00
    direction = residual + beta * start
    moved = (alpha * mean + beta) * image - alpha * second + noise_level * direction
    quad = alpha * alpha * (b12 - 2.0 * mean * b11 + mean * mean * b01)
    mixed = alpha * (mean * b01 - b11)
    curve = quad + 2.0 * beta * mixed + beta * beta * b01
    curve = curve + noise_level * (now + beta * beta * b00)
    step = now / curve
    sol_ref[...] = alpha * start + step * direction
    res_ref[...] = residual - step * moved


def shards(features, lengthscale, targets, mask):
    rows, ys, cores = (lax.axis_size(name) for name in ("row", "y", "core"))
    cols = ys * cores
    epochs, width = targets.shape
    feat = features.shape[0]
    total_count = width * rows * cols
    field = jax.ShapeDtypeStruct((epochs, width), f32)
    sums_shape = jax.ShapeDtypeStruct((1, 128), f32)
    half_shape = jax.ShapeDtypeStruct((ys, epochs, width), f32)
    half_more = jax.ShapeDtypeStruct((ys, epochs + 8, width), f32)
    part_scratch = pltpu.VMEM((cols, epochs, width), f32)
    away = pl.BlockSpec(memory_space=pl.ANY)
    hbm = pl.BlockSpec(memory_space=pltpu.HBM)
    pack_rows = 2 * feat + epochs

    feats, pack = pl.pallas_call(
        functools.partial(prepare_kernel, total_count),
        out_shape=(
            jax.ShapeDtypeStruct((2 * feat, width), bf16),
            jax.ShapeDtypeStruct((rows, pack_rows, width), bf16),
        ),
        in_specs=[hbm, VMEM, hbm, hbm],
        out_specs=[VMEM, away],
        scratch_shapes=[
            pltpu.VMEM((feat, width), f32),
            pltpu.VMEM((epochs, width), f32),
            pltpu.VMEM((epochs, width), jnp.int32),
            pltpu.VMEM((pack_rows, width), bf16),
            pltpu.SemaphoreType.DMA((rows,)),
            pltpu.SemaphoreType.DMA((3,)),
        ],
        compiler_params=params(60),
    )(features, lengthscale[None, :], targets, mask)

    col_pack = lax.all_to_all(pack, "row", 0, 0)
    row_feats = lax.all_gather(feats, COL)

    step_rows = 768
    depth = 4 * feat + 16
    tail = AGAIN * step_rows
    tile, right, left, mine, other = pl.pallas_call(
        functools.partial(block_kernel, step_rows),
        grid=(rows * width // step_rows,),
        out_shape=(
            jax.ShapeDtypeStruct((rows * width, cols * width), bf16),
            jax.ShapeDtypeStruct((depth, cols * width), bf16),
            jax.ShapeDtypeStruct((depth, tail), bf16),
            half_shape,
            half_shape,
        ),
        in_specs=[VMEM] * 2,
        out_specs=[pl.BlockSpec((step_rows, cols * width), lambda s: (s, 0))] + [VMEM] * 4,
        scratch_shapes=[
            pltpu.VMEM((depth, rows * width), bf16),
            pltpu.VMEM((epochs, rows * width), bf16),
            part_scratch,
        ],
        compiler_params=params(48),
    )(row_feats, col_pack)

    terms = exchange(pair_sum(mine, other, field))
    image, pack, sums = pl.pallas_call(
        functools.partial(middle_kernel, total_count),
        out_shape=(field, jax.ShapeDtypeStruct((rows, epochs, width), bf16), sums_shape),
        in_specs=[VMEM] * (len(terms) + 2),
        out_specs=[VMEM, away, VMEM],
        scratch_shapes=[
            pltpu.VMEM((epochs, width), bf16),
            pltpu.SemaphoreType.DMA((rows,)),
        ],
        compiler_params=params(8),
    )(*terms, targets, mask)
    col_weighted = lax.all_to_all(pack, "row", 0, 0)
    row_images = lax.all_gather(image, COL)

    again_rows = 768
    held_rows = rows * width - tail
    mine, other = pl.pallas_call(
        functools.partial(again_kernel, again_rows),
        out_shape=(half_more,) * 2,
        in_specs=[away] + [VMEM] * 5,
        out_specs=[VMEM] * 2,
        scratch_shapes=[
            pltpu.VMEM((held_rows, cols * width), bf16),
            pltpu.VMEM((epochs, rows * width), bf16),
            part_scratch,
            pltpu.SemaphoreType.DMA((held_rows // again_rows,)),
        ],
        compiler_params=params(50),
    )(tile, right, left, col_weighted, row_images, sums)

    *terms, sums = pair_sum(
        mine, other, field, jax.ShapeDtypeStruct((rows * ys, FAT, 128), f32)
    )
    sums = lax.all_to_all(sums, ("row", "y"), 0, 0)
    terms = exchange(terms)
    return pl.pallas_call(
        finish_kernel,
        out_shape=(field, field),
        in_specs=[VMEM] * (len(terms) + 4),
        out_specs=[VMEM] * 2,
        compiler_params=params(8),
    )(*terms, sums, image, targets, mask)


def solution(mesh):
    rows, cols = mesh.devices.shape
    split = jax.sharding.Mesh(mesh.devices.reshape(rows, cols // 2, 2), ("row",) + COL)
    whole = P(None, ("row",) + COL)
    return jax.shard_map(
        shards,
        mesh=split,
        in_specs=(whole, P(), whole, whole),
        out_specs=(whole, whole),
        check_vma=False,
    )
```

```python
import functools
import math

import jax
import jax.numpy as jnp
from jax import lax
from jax.experimental import pallas as pl
from jax.experimental.pallas import tpu as pltpu
from jax.sharding import PartitionSpec as P

noise_level = 0.5
AGAIN = 2
FAT = 8
COL = ("y", "core")
VMEM = pl.BlockSpec(memory_space=pltpu.VMEM)
bf16 = jnp.bfloat16
f32 = jnp.float32


def params(mib, **more):
    return pltpu.CompilerParams(vmem_limit_bytes=mib << 20, **more)


def epoch_kernel(epochs, total_count):
    s = lax.broadcasted_iota(jnp.int32, (epochs, epochs), 0)
    t = lax.broadcasted_iota(jnp.int32, (epochs, epochs), 1)
    gap = jnp.abs(s - t).astype(f32)
    return (8.0 / math.sqrt(total_count)) * jnp.exp(-gap / (epochs / 4.0))


def epoch_product(field, total_count):
    kernel_t = epoch_kernel(field.shape[0], total_count)
    return jnp.dot(
        kernel_t, field, precision=lax.Precision.HIGHEST, preferred_element_type=f32
    )


def prepare_kernel(
    total_count, feat_in, scale_in, target_in, mask_in, feats_ref, out_ref,
    feat_ref, scale_ref, target_ref, mask_ref, pack, sem, feats_sem, load_sem,
):
    loads = [
        pltpu.make_async_copy(source, target, load_sem.at[place])
        for place, (source, target) in enumerate(
            (
                (scale_in, scale_ref),
                (feat_in, feat_ref),
                (target_in, target_ref),
                (mask_in, mask_ref),
            )
        )
    ]
    for load in loads:
        load.start()
    count = feat_ref.shape[0]
    loads[0].wait()
    across = lax.broadcasted_iota(jnp.int32, (count, count), 0)
    down = lax.broadcasted_iota(jnp.int32, (count, count), 1)
    scale = jnp.sum(jnp.where(across == down, scale_ref[...], 0.0), axis=1, keepdims=True)
    loads[1].wait()
    scaled = feat_ref[...] / scale * math.sqrt(math.log2(math.e))
    high = scaled.astype(bf16)
    low = (scaled - high.astype(f32)).astype(bf16)
    pack[0:count, :] = high
    pack[count : 2 * count, :] = low
    feats_copy = pltpu.make_async_copy(pack.at[0 : 2 * count], feats_ref, feats_sem)
    feats_copy.start()
    loads[2].wait()
    loads[3].wait()
    start = target_ref[...] * mask_ref[...].astype(f32)
    pack[2 * count :, :] = epoch_product(start, total_count).astype(bf16)
    send_all(pack, out_ref, sem)
    feats_copy.wait()


def send_all(source, out_ref, sem):
    copies = [
        pltpu.make_async_copy(source, out_ref.at[place], sem.at[place])
        for place in range(out_ref.shape[0])
    ]
    for copy in copies:
        copy.start()
    for copy in copies:
        copy.wait()


def norm_parts(feats):
    count = feats.shape[0] // 2
    whole = feats[:count, :].astype(f32) + feats[count:, :].astype(f32)
    norm = -0.5 * jnp.sum(whole * whole, axis=0, keepdims=True)
    first = norm.astype(bf16).astype(f32)
    second = (norm - first).astype(bf16).astype(f32)
    third = norm - first - second
    return first, second, third


def block_kernel(
    step_rows, row_ref, col_ref, tile_ref, right, tail_ref, mine_ref, other_ref,
    left, fields, part_ref,
):
    step = pl.program_id(0)
    blocks, epochs, width = part_ref.shape
    count = row_ref.shape[1] // 2
    total = part_ref

    def rows(*parts):
        blank = jnp.zeros((16 - len(parts), width), f32)
        return jnp.concatenate(list(parts) + [blank], axis=0).astype(bf16)

    @pl.when(step == 0)
    def _():
        one = jnp.ones((1, width), f32)
        for block in range(row_ref.shape[0]):
            at = slice(block * width, (block + 1) * width)
            feats = row_ref[block]
            first, second, third = norm_parts(feats)
            right[0 : 2 * count, at] = feats
            right[2 * count : 4 * count, at] = feats
            right[4 * count :, at] = rows(one, one, one, first, second, third)
        for block in range(col_ref.shape[0]):
            at = slice(block * width, (block + 1) * width)
            feats = col_ref[block, 0 : 2 * count, :]
            first, second, third = norm_parts(feats)
            high = feats[0:count, :]
            low = feats[count:, :]
            left[0:count, at] = high
            left[count : 2 * count, at] = high
            left[2 * count : 3 * count, at] = low
            left[3 * count : 4 * count, at] = low
            left[4 * count :, at] = rows(first, second, third, one, one, one)
            fields[:, at] = col_ref[block, 2 * count :, :]
        part_ref[...] = jnp.zeros_like(part_ref)
        tail_ref[...] = left[:, left.shape[1] - tail_ref.shape[1] :]

    at = pl.ds(pl.multiple_of(step * step_rows, step_rows), step_rows)
    power = lax.dot_general(
        left[:, at], right[...], (((0,), (0,)), ((), ())), preferred_element_type=f32
    )
    tile = jnp.exp2(power).astype(bf16)
    tile_ref[...] = tile
    spread = jnp.dot(fields[:, at], tile, preferred_element_type=f32)
    for block in range(blocks):
        part_ref[block] += spread[:, block * width : (block + 1) * width]

    @pl.when(step == pl.num_programs(0) - 1)
    def _():
        split_parts(part_ref, mine_ref, other_ref)


def split_parts(part_ref, mine_ref, other_ref):
    core = lax.axis_index("core")
    epochs = part_ref.shape[1]
    for place in range(mine_ref.shape[0]):
        mine_ref[place, 0:epochs, :] = part_ref[2 * place + core]
        other_ref[place, 0:epochs, :] = part_ref[2 * place + 1 - core]


def add_kernel(mine_ref, other_ref, *out_refs):
    count = mine_ref.shape[0]
    epochs = out_refs[0].shape[0]
    here = lax.axis_index("y")
    for shift, out_ref in enumerate(out_refs[:count]):
        place = lax.rem(here + shift, count)
        out_ref[...] = mine_ref[place, 0:epochs, :] + other_ref[place, 0:epochs, :]
    for sums_ref in out_refs[count:]:
        row = mine_ref[0, epochs:, 0:128] + other_ref[0, epochs:, 0:128]
        sums_ref[...] = jnp.broadcast_to(row[None], sums_ref.shape)


def pair_sum(mine, other, block, *more):
    count = mine.shape[0]
    other = lax.ppermute(other, "core", [(0, 1), (1, 0)])
    return pl.pallas_call(
        add_kernel,
        out_shape=(block,) * count + more,
        in_specs=[VMEM] * 2,
        out_specs=[VMEM] * (count + len(more)),
        compiler_params=params(8),
    )(mine, other)


def exchange(terms):
    count = len(terms)
    return [
        lax.ppermute(term, "y", [(k, (k + shift) % count) for k in range(count)])
        if shift
        else term
        for shift, term in enumerate(terms)
    ]


def middle_kernel(
    total_count, *refs
):
    *part_refs, target_ref, mask_ref, image_ref, out_ref, sums_ref, pack, sem = refs
    observed = mask_ref[...].astype(f32)
    start = target_ref[...] * observed
    image = observed * sum(part_ref[...] for part_ref in part_refs)
    image_ref[...] = image
    pack[...] = epoch_product(image, total_count).astype(bf16)
    send_all(pack, out_ref, sem)
    sums_ref[...] = lanes(
        jnp.sum(start * start), jnp.sum(start * image), jnp.sum(image * image)
    )


def lanes(*values):
    lane = lax.broadcasted_iota(jnp.int32, (1, 128), 1)
    row = jnp.zeros((1, 128), f32)
    for place, value in enumerate(values):
        row = jnp.where(lane == place, value, row)
    return row


def again_kernel(
    step_rows, tile_ref, right_ref, left_ref, col_ref, image_ref, sums_ref, mine_ref, other_ref,
    held, fields, part_ref, sem,
):
    blocks, epochs, width = part_ref.shape
    steps = held.shape[0] // step_rows

    def load(step):
        at = pl.ds(pl.multiple_of(step * step_rows, step_rows), step_rows)
        return pltpu.make_async_copy(tile_ref.at[at], held.at[at], sem.at[step])

    for step in range(steps):
        load(step).start()
    for block in range(col_ref.shape[0]):
        fields[:, block * width : (block + 1) * width] = col_ref[block]
    part_ref[...] = jnp.zeros_like(part_ref)

    def add(at, tile):
        spread = jnp.dot(fields[:, at], tile, preferred_element_type=f32)
        for block in range(blocks):
            part_ref[block] += spread[:, block * width : (block + 1) * width]

    def again(step, carry):
        at = pl.ds(pl.multiple_of(step * step_rows, step_rows), step_rows)
        power = lax.dot_general(
            left_ref[:, at], right_ref[...], (((0,), (0,)), ((), ())), preferred_element_type=f32
        )
        at = pl.ds(pl.multiple_of(held.shape[0] + step * step_rows, step_rows), step_rows)
        add(at, jnp.exp2(power).astype(bf16))
        return carry

    def body(step, carry):
        load(step).wait()
        at = pl.ds(pl.multiple_of(step * step_rows, step_rows), step_rows)
        add(at, held[at, :])
        return carry

    lax.fori_loop(0, left_ref.shape[1] // step_rows, again, 0)

    lax.fori_loop(0, steps, body, 0)
    split_parts(part_ref, mine_ref, other_ref)
    cross = jnp.zeros((epochs, width), f32)
    for block in range(blocks):
        cross = cross + part_ref[block] * image_ref[block]
    row = sums_ref[...] + lanes(0.0, 0.0, 0.0, jnp.sum(cross))
    for half_ref in (mine_ref, other_ref):
        half_ref[0, epochs:, 0:128] = jnp.broadcast_to(row, (8, 128))


def finish_kernel(*refs):
    *part_refs, sums_ref, image_ref, target_ref, mask_ref, sol_ref, res_ref = refs
    observed = mask_ref[...].astype(f32)
    start = target_ref[...] * observed
    image = image_ref[...]
    second = observed * sum(part_ref[...] for part_ref in part_refs)
    totals = jnp.sum(sums_ref[...], axis=0)[0:1]
    b00, b01 = totals[:, 0:1], totals[:, 1:2]
    b11, b12 = totals[:, 2:3], totals[:, 3:4]
    mean = b01 / b00
    alpha = 1.0 / (mean + noise_level)
    residual = alpha * (mean * start - image)
    now = alpha * alpha * (b11 - mean * b01)
    beta = now / b00
    direction = residual + beta * start
    moved = (alpha * mean + beta) * image - alpha * second + noise_level * direction
    quad = alpha * alpha * (b12 - 2.0 * mean * b11 + mean * mean * b01)
    mixed = alpha * (mean * b01 - b11)
    curve = quad + 2.0 * beta * mixed + beta * beta * b01
    curve = curve + noise_level * (now + beta * beta * b00)
    step = now / curve
    sol_ref[...] = alpha * start + step * direction
    res_ref[...] = residual - step * moved


def shards(features, lengthscale, targets, mask):
    rows, ys, cores = (lax.axis_size(name) for name in ("row", "y", "core"))
    cols = ys * cores
    epochs, width = targets.shape
    feat = features.shape[0]
    total_count = width * rows * cols
    field = jax.ShapeDtypeStruct((epochs, width), f32)
    sums_shape = jax.ShapeDtypeStruct((1, 128), f32)
    half_shape = jax.ShapeDtypeStruct((ys, epochs, width), f32)
    half_more = jax.ShapeDtypeStruct((ys, epochs + 8, width), f32)
    part_scratch = pltpu.VMEM((cols, epochs, width), f32)
    away = pl.BlockSpec(memory_space=pl.ANY)
    hbm = pl.BlockSpec(memory_space=pltpu.HBM)
    pack_rows = 2 * feat + epochs

    feats, pack = pl.pallas_call(
        functools.partial(prepare_kernel, total_count),
        out_shape=(
            jax.ShapeDtypeStruct((2 * feat, width), bf16),
            jax.ShapeDtypeStruct((rows, pack_rows, width), bf16),
        ),
        in_specs=[hbm] * 4,
        out_specs=[away, away],
        scratch_shapes=[
            pltpu.VMEM((feat, width), f32),
            pltpu.VMEM((1, feat), f32),
            pltpu.VMEM((epochs, width), f32),
            pltpu.VMEM((epochs, width), jnp.int32),
            pltpu.VMEM((pack_rows, width), bf16),
            pltpu.SemaphoreType.DMA((rows,)),
            pltpu.SemaphoreType.DMA,
            pltpu.SemaphoreType.DMA((4,)),
        ],
        compiler_params=params(60),
    )(features, lengthscale[None, :], targets, mask)

    col_pack = lax.all_to_all(pack, "row", 0, 0)
    row_feats = lax.all_gather(feats, COL)

    step_rows = 768
    depth = 4 * feat + 16
    tail = AGAIN * step_rows
    tile, right, left, mine, other = pl.pallas_call(
        functools.partial(block_kernel, step_rows),
        grid=(rows * width // step_rows,),
        out_shape=(
            jax.ShapeDtypeStruct((rows * width, cols * width), bf16),
            jax.ShapeDtypeStruct((depth, cols * width), bf16),
            jax.ShapeDtypeStruct((depth, tail), bf16),
            half_shape,
            half_shape,
        ),
        in_specs=[VMEM] * 2,
        out_specs=[pl.BlockSpec((step_rows, cols * width), lambda s: (s, 0))] + [VMEM] * 4,
        scratch_shapes=[
            pltpu.VMEM((depth, rows * width), bf16),
            pltpu.VMEM((epochs, rows * width), bf16),
            part_scratch,
        ],
        compiler_params=params(48),
    )(row_feats, col_pack)

    terms = exchange(pair_sum(mine, other, field))
    image, pack, sums = pl.pallas_call(
        functools.partial(middle_kernel, total_count),
        out_shape=(field, jax.ShapeDtypeStruct((rows, epochs, width), bf16), sums_shape),
        in_specs=[VMEM] * (len(terms) + 2),
        out_specs=[VMEM, away, VMEM],
        scratch_shapes=[
            pltpu.VMEM((epochs, width), bf16),
            pltpu.SemaphoreType.DMA((rows,)),
        ],
        compiler_params=params(8),
    )(*terms, targets, mask)
    col_weighted = lax.all_to_all(pack, "row", 0, 0)
    row_images = lax.all_gather(image, COL)

    again_rows = 768
    held_rows = rows * width - tail
    mine, other = pl.pallas_call(
        functools.partial(again_kernel, again_rows),
        out_shape=(half_more,) * 2,
        in_specs=[away] + [VMEM] * 5,
        out_specs=[VMEM] * 2,
        scratch_shapes=[
            pltpu.VMEM((held_rows, cols * width), bf16),
            pltpu.VMEM((epochs, rows * width), bf16),
            part_scratch,
            pltpu.SemaphoreType.DMA((held_rows // again_rows,)),
        ],
        compiler_params=params(50),
    )(tile, right, left, col_weighted, row_images, sums)

    *terms, sums = pair_sum(
        mine, other, field, jax.ShapeDtypeStruct((rows * ys, FAT, 128), f32)
    )
    sums = lax.all_to_all(sums, ("row", "y"), 0, 0)
    terms = exchange(terms)
    return pl.pallas_call(
        finish_kernel,
        out_shape=(field, field),
        in_specs=[VMEM] * (len(terms) + 4),
        out_specs=[VMEM] * 2,
        compiler_params=params(8),
    )(*terms, sums, image, targets, mask)


def solution(mesh):
    rows, cols = mesh.devices.shape
    split = jax.sharding.Mesh(mesh.devices.reshape(rows, cols // 2, 2), ("row",) + COL)
    whole = P(None, ("row",) + COL)
    return jax.shard_map(
        shards,
        mesh=split,
        in_specs=(whole, P(), whole, whole),
        out_specs=(whole, whole),
        check_vma=False,
    )
```

```python
import functools
import math

import jax
import jax.numpy as jnp
from jax import lax
from jax.experimental import pallas as pl
from jax.experimental.pallas import tpu as pltpu
from jax.sharding import PartitionSpec as P

noise_level = 0.5
AGAIN = 2
SUM_ROWS = 4
COL = ("y", "core")
VMEM = pl.BlockSpec(memory_space=pltpu.VMEM)
bf16 = jnp.bfloat16
f32 = jnp.float32


def params(mib, **more):
    return pltpu.CompilerParams(vmem_limit_bytes=mib << 20, **more)


def epoch_kernel(epochs, total_count):
    s = lax.broadcasted_iota(jnp.int32, (epochs, epochs), 0)
    t = lax.broadcasted_iota(jnp.int32, (epochs, epochs), 1)
    gap = jnp.abs(s - t).astype(f32)
    return (8.0 / math.sqrt(total_count)) * jnp.exp(-gap / (epochs / 4.0))


def epoch_product(field, total_count):
    kernel_t = epoch_kernel(field.shape[0], total_count)
    return jnp.dot(
        kernel_t, field, precision=lax.Precision.HIGHEST, preferred_element_type=f32
    )


def prepare_kernel(
    total_count, feat_in, scale_in, target_in, mask_in, feats_ref, out_ref,
    feat_ref, scale_ref, target_ref, mask_ref, pack, sem, feats_sem, load_sem,
):
    loads = [
        pltpu.make_async_copy(source, target, load_sem.at[place])
        for place, (source, target) in enumerate(
            (
                (scale_in, scale_ref),
                (feat_in, feat_ref),
                (target_in, target_ref),
                (mask_in, mask_ref),
            )
        )
    ]
    for load in loads:
        load.start()
    count = feat_ref.shape[0]
    loads[0].wait()
    across = lax.broadcasted_iota(jnp.int32, (count, count), 0)
    down = lax.broadcasted_iota(jnp.int32, (count, count), 1)
    scale = jnp.sum(jnp.where(across == down, scale_ref[...], 0.0), axis=1, keepdims=True)
    loads[1].wait()
    scaled = feat_ref[...] / scale * math.sqrt(math.log2(math.e))
    high = scaled.astype(bf16)
    low = (scaled - high.astype(f32)).astype(bf16)
    pack[0:count, :] = high
    pack[count : 2 * count, :] = low
    feats_copy = pltpu.make_async_copy(pack.at[0 : 2 * count], feats_ref, feats_sem)
    feats_copy.start()
    loads[2].wait()
    loads[3].wait()
    start = target_ref[...] * mask_ref[...].astype(f32)
    pack[2 * count :, :] = epoch_product(start, total_count).astype(bf16)
    send_all(pack, out_ref, sem)
    feats_copy.wait()


def send_all(source, out_ref, sem):
    copies = [
        pltpu.make_async_copy(source, out_ref.at[place], sem.at[place])
        for place in range(out_ref.shape[0])
    ]
    for copy in copies:
        copy.start()
    for copy in copies:
        copy.wait()


def norm_parts(feats):
    count = feats.shape[0] // 2
    whole = feats[:count, :].astype(f32) + feats[count:, :].astype(f32)
    norm = -0.5 * jnp.sum(whole * whole, axis=0, keepdims=True)
    first = norm.astype(bf16).astype(f32)
    second = (norm - first).astype(bf16).astype(f32)
    third = norm - first - second
    return first, second, third


def block_kernel(
    step_rows, row_ref, col_ref, tile_ref, right, tail_ref, mine_ref, other_ref,
    left, fields, part_ref,
):
    step = pl.program_id(0)
    blocks, epochs, width = part_ref.shape
    count = row_ref.shape[1] // 2
    total = part_ref

    def rows(*parts):
        blank = jnp.zeros((16 - len(parts), width), f32)
        return jnp.concatenate(list(parts) + [blank], axis=0).astype(bf16)

    @pl.when(step == 0)
    def _():
        one = jnp.ones((1, width), f32)
        for block in range(row_ref.shape[0]):
            at = slice(block * width, (block + 1) * width)
            feats = row_ref[block]
            first, second, third = norm_parts(feats)
            right[0 : 2 * count, at] = feats
            right[2 * count : 4 * count, at] = feats
            right[4 * count :, at] = rows(one, one, one, first, second, third)
        for block in range(col_ref.shape[0]):
            at = slice(block * width, (block + 1) * width)
            feats = col_ref[block, 0 : 2 * count, :]
            first, second, third = norm_parts(feats)
            high = feats[0:count, :]
            low = feats[count:, :]
            left[0:count, at] = high
            left[count : 2 * count, at] = high
            left[2 * count : 3 * count, at] = low
            left[3 * count : 4 * count, at] = low
            left[4 * count :, at] = rows(first, second, third, one, one, one)
            fields[:, at] = col_ref[block, 2 * count :, :]
        part_ref[...] = jnp.zeros_like(part_ref)
        tail_ref[...] = left[:, left.shape[1] - tail_ref.shape[1] :]

    at = pl.ds(pl.multiple_of(step * step_rows, step_rows), step_rows)
    power = lax.dot_general(
        left[:, at], right[...], (((0,), (0,)), ((), ())), preferred_element_type=f32
    )
    tile = jnp.exp2(power).astype(bf16)
    tile_ref[...] = tile
    spread = jnp.dot(fields[:, at], tile, preferred_element_type=f32)
    for block in range(blocks):
        part_ref[block] += spread[:, block * width : (block + 1) * width]

    @pl.when(step == pl.num_programs(0) - 1)
    def _():
        split_parts(part_ref, mine_ref, other_ref)


def split_parts(part_ref, mine_ref, other_ref):
    core = lax.axis_index("core")
    epochs = part_ref.shape[1]
    for place in range(mine_ref.shape[0]):
        mine_ref[place, 0:epochs, :] = part_ref[2 * place + core]
        other_ref[place, 0:epochs, :] = part_ref[2 * place + 1 - core]


def add_kernel(mine_ref, other_ref, *out_refs):
    count = mine_ref.shape[0]
    epochs = out_refs[0].shape[0]
    here = lax.axis_index("y")
    for shift, out_ref in enumerate(out_refs[:count]):
        place = lax.rem(here + shift, count)
        out_ref[...] = mine_ref[place, 0:epochs, :] + other_ref[place, 0:epochs, :]
    for sums_ref in out_refs[count:]:
        row = mine_ref[0, epochs:, 0:128] + other_ref[0, epochs:, 0:128]
        sums_ref[...] = jnp.broadcast_to(row[None, 0:SUM_ROWS], sums_ref.shape)


def pair_sum(mine, other, block, *more):
    count = mine.shape[0]
    other = lax.ppermute(other, "core", [(0, 1), (1, 0)])
    return pl.pallas_call(
        add_kernel,
        out_shape=(block,) * count + more,
        in_specs=[VMEM] * 2,
        out_specs=[VMEM] * (count + len(more)),
        compiler_params=params(8),
    )(mine, other)


def exchange(terms):
    count = len(terms)
    return [
        lax.ppermute(term, "y", [(k, (k + shift) % count) for k in range(count)])
        if shift
        else term
        for shift, term in enumerate(terms)
    ]


def middle_kernel(
    total_count, *refs
):
    *part_refs, target_ref, mask_ref, image_ref, out_ref, sums_ref, pack, sem = refs
    observed = mask_ref[...].astype(f32)
    start = target_ref[...] * observed
    image = observed * sum(part_ref[...] for part_ref in part_refs)
    image_ref[...] = image
    pack[...] = epoch_product(image, total_count).astype(bf16)
    send_all(pack, out_ref, sem)
    sums_ref[...] = lanes(
        jnp.sum(start * start), jnp.sum(start * image), jnp.sum(image * image)
    )


def lanes(*values):
    lane = lax.broadcasted_iota(jnp.int32, (1, 128), 1)
    row = jnp.zeros((1, 128), f32)
    for place, value in enumerate(values):
        row = jnp.where(lane == place, value, row)
    return row


def again_kernel(
    step_rows, tile_ref, right_ref, left_ref, col_ref, image_ref, sums_ref, mine_ref, other_ref,
    held, fields, part_ref, sem,
):
    blocks, epochs, width = part_ref.shape
    steps = held.shape[0] // step_rows

    def load(step):
        at = pl.ds(pl.multiple_of(step * step_rows, step_rows), step_rows)
        return pltpu.make_async_copy(tile_ref.at[at], held.at[at], sem.at[step])

    for step in range(steps):
        load(step).start()
    for block in range(col_ref.shape[0]):
        fields[:, block * width : (block + 1) * width] = col_ref[block]
    part_ref[...] = jnp.zeros_like(part_ref)

    def add(at, tile):
        spread = jnp.dot(fields[:, at], tile, preferred_element_type=f32)
        for block in range(blocks):
            part_ref[block] += spread[:, block * width : (block + 1) * width]

    def again(step, carry):
        at = pl.ds(pl.multiple_of(step * step_rows, step_rows), step_rows)
        power = lax.dot_general(
            left_ref[:, at], right_ref[...], (((0,), (0,)), ((), ())), preferred_element_type=f32
        )
        at = pl.ds(pl.multiple_of(held.shape[0] + step * step_rows, step_rows), step_rows)
        add(at, jnp.exp2(power).astype(bf16))
        return carry

    def body(step, carry):
        load(step).wait()
        at = pl.ds(pl.multiple_of(step * step_rows, step_rows), step_rows)
        add(at, held[at, :])
        return carry

    lax.fori_loop(0, left_ref.shape[1] // step_rows, again, 0)

    lax.fori_loop(0, steps, body, 0)
    split_parts(part_ref, mine_ref, other_ref)
    cross = jnp.zeros((epochs, width), f32)
    for block in range(blocks):
        cross = cross + part_ref[block] * image_ref[block]
    row = sums_ref[...] + lanes(0.0, 0.0, 0.0, jnp.sum(cross))
    for half_ref in (mine_ref, other_ref):
        half_ref[0, epochs:, 0:128] = jnp.broadcast_to(row, (8, 128))


def finish_kernel(*refs):
    *part_refs, sums_ref, image_ref, target_ref, mask_ref, sol_ref, res_ref = refs
    observed = mask_ref[...].astype(f32)
    start = target_ref[...] * observed
    image = image_ref[...]
    second = observed * sum(part_ref[...] for part_ref in part_refs)
    totals = jnp.sum(sums_ref[...], axis=0)[0:1]
    b00, b01 = totals[:, 0:1], totals[:, 1:2]
    b11, b12 = totals[:, 2:3], totals[:, 3:4]
    mean = b01 / b00
    alpha = 1.0 / (mean + noise_level)
    residual = alpha * (mean * start - image)
    now = alpha * alpha * (b11 - mean * b01)
    beta = now / b00
    direction = residual + beta * start
    moved = (alpha * mean + beta) * image - alpha * second + noise_level * direction
    quad = alpha * alpha * (b12 - 2.0 * mean * b11 + mean * mean * b01)
    mixed = alpha * (mean * b01 - b11)
    curve = quad + 2.0 * beta * mixed + beta * beta * b01
    curve = curve + noise_level * (now + beta * beta * b00)
    step = now / curve
    sol_ref[...] = alpha * start + step * direction
    res_ref[...] = residual - step * moved


def shards(features, lengthscale, targets, mask):
    rows, ys, cores = (lax.axis_size(name) for name in ("row", "y", "core"))
    cols = ys * cores
    epochs, width = targets.shape
    feat = features.shape[0]
    total_count = width * rows * cols
    field = jax.ShapeDtypeStruct((epochs, width), f32)
    sums_shape = jax.ShapeDtypeStruct((1, 128), f32)
    half_shape = jax.ShapeDtypeStruct((ys, epochs, width), f32)
    half_more = jax.ShapeDtypeStruct((ys, epochs + 8, width), f32)
    part_scratch = pltpu.VMEM((cols, epochs, width), f32)
    away = pl.BlockSpec(memory_space=pl.ANY)
    hbm = pl.BlockSpec(memory_space=pltpu.HBM)
    pack_rows = 2 * feat + epochs

    feats, pack = pl.pallas_call(
        functools.partial(prepare_kernel, total_count),
        out_shape=(
            jax.ShapeDtypeStruct((2 * feat, width), bf16),
            jax.ShapeDtypeStruct((rows, pack_rows, width), bf16),
        ),
        in_specs=[hbm] * 4,
        out_specs=[away, away],
        scratch_shapes=[
            pltpu.VMEM((feat, width), f32),
            pltpu.VMEM((1, feat), f32),
            pltpu.VMEM((epochs, width), f32),
            pltpu.VMEM((epochs, width), jnp.int32),
            pltpu.VMEM((pack_rows, width), bf16),
            pltpu.SemaphoreType.DMA((rows,)),
            pltpu.SemaphoreType.DMA,
            pltpu.SemaphoreType.DMA((4,)),
        ],
        compiler_params=params(60),
    )(features, lengthscale[None, :], targets, mask)

    col_pack = lax.all_to_all(pack, "row", 0, 0)
    row_feats = lax.all_gather(feats, COL)

    step_rows = 768
    depth = 4 * feat + 16
    tail = AGAIN * step_rows
    tile, right, left, mine, other = pl.pallas_call(
        functools.partial(block_kernel, step_rows),
        grid=(rows * width // step_rows,),
        out_shape=(
            jax.ShapeDtypeStruct((rows * width, cols * width), bf16),
            jax.ShapeDtypeStruct((depth, cols * width), bf16),
            jax.ShapeDtypeStruct((depth, tail), bf16),
            half_shape,
            half_shape,
        ),
        in_specs=[VMEM] * 2,
        out_specs=[pl.BlockSpec((step_rows, cols * width), lambda s: (s, 0))] + [VMEM] * 4,
        scratch_shapes=[
            pltpu.VMEM((depth, rows * width), bf16),
            pltpu.VMEM((epochs, rows * width), bf16),
            part_scratch,
        ],
        compiler_params=params(48),
    )(row_feats, col_pack)

    terms = exchange(pair_sum(mine, other, field))
    image, pack, sums = pl.pallas_call(
        functools.partial(middle_kernel, total_count),
        out_shape=(field, jax.ShapeDtypeStruct((rows, epochs, width), bf16), sums_shape),
        in_specs=[VMEM] * (len(terms) + 2),
        out_specs=[VMEM, away, VMEM],
        scratch_shapes=[
            pltpu.VMEM((epochs, width), bf16),
            pltpu.SemaphoreType.DMA((rows,)),
        ],
        compiler_params=params(8),
    )(*terms, targets, mask)
    col_weighted = lax.all_to_all(pack, "row", 0, 0)
    row_images = lax.all_gather(image, COL)

    again_rows = 768
    held_rows = rows * width - tail
    mine, other = pl.pallas_call(
        functools.partial(again_kernel, again_rows),
        out_shape=(half_more,) * 2,
        in_specs=[away] + [VMEM] * 5,
        out_specs=[VMEM] * 2,
        scratch_shapes=[
            pltpu.VMEM((held_rows, cols * width), bf16),
            pltpu.VMEM((epochs, rows * width), bf16),
            part_scratch,
            pltpu.SemaphoreType.DMA((held_rows // again_rows,)),
        ],
        compiler_params=params(50),
    )(tile, right, left, col_weighted, row_images, sums)

    *terms, sums = pair_sum(
        mine, other, field, jax.ShapeDtypeStruct((rows * ys, SUM_ROWS, 128), f32)
    )
    sums = lax.all_to_all(sums, ("row", "y"), 0, 0)
    terms = exchange(terms)
    return pl.pallas_call(
        finish_kernel,
        out_shape=(field, field),
        in_specs=[VMEM] * (len(terms) + 4),
        out_specs=[VMEM] * 2,
        compiler_params=params(8),
    )(*terms, sums, image, targets, mask)


def solution(mesh):
    rows, cols = mesh.devices.shape
    split = jax.sharding.Mesh(mesh.devices.reshape(rows, cols // 2, 2), ("row",) + COL)
    whole = P(None, ("row",) + COL)
    return jax.shard_map(
        shards,
        mesh=split,
        in_specs=(whole, P(), whole, whole),
        out_specs=(whole, whole),
        check_vma=False,
    )
```
